128 devices in a mesh: dp: 8 (over y, core), layer: 4 (over z), query: 4 (over x).
Axes of the slice: x: 4, y: 4, z: 4, core: 2. Of those that a mesh axis runs over, the one named last changes fastest.
Arguments:
- train_grad: bfloat16 [16384, 4, 4096], P('dp', 'layer'), may hold values from -6 to 6
- query_grad: bfloat16 [16, 128, 4, 4096], P('query', None, 'layer'), may hold values from -0.046875 to 0.046875
- sketch: bfloat16 [512, 4, 4096], P('dp', 'layer')
- pairs: int32 [1536, 2], P(('dp', 'query')), may hold values from 0 to 127, as said below
- counts: int32 [128], P('dp'), may hold values from 32 to 128, as said below
Outputs:
- scores: float32 [1536, 128, 128], P(('dp', 'query'), 'layer')
The draws below stay inside these ranges and needn't reach their ends.
Inputs may be any that keep to these rules, and one draw needn't show every extreme that they name: `pairs`: rows g * 192 to (g + 1) * 192 - 1 name only train blocks g * 16 to (g + 1) * 16 - 1; column 0 is below 128, column 1 is a query block below 16; no pair appears twice. `counts`: among the 16 blocks g * 16 to (g + 1) * 16 - 1 at least one holds 128 examples.
All inputs are finite; a program needn't handle non-finite values.
Results may differ from the reference program's by a relative error of at most 0.0031.
Values may be sent and summed in bfloat16 or wider, within the bound.
No kernel may reach another device: no remote copies, remote signals or barrier semaphores. Data moves between devices by JAX's collectives and lax.ppermute only.
A program may use at most 192 MiB of HBM per device.

```python
import jax
import jax.numpy as jnp
from jax import lax

F = 4096
K = 512
TB = 128
QB = 128
TBLK_DEV = 16
LAYERS = 4
TBLOCKS = 128
TRAIN = 16384
QBLOCKS = 16
NQ = 2048
PAIRS_GROUP = 192
NPAIRS = 1536


def draw_sketch(key, part):
    key = jax.random.fold_in(key, 7)
    row_pos = jnp.arange(K, dtype=jnp.float32) / K
    row_scale = jnp.sqrt(20.0 / K * jnp.exp(-2.2 * row_pos))
    values = jax.random.normal(key, (K, LAYERS, F), jnp.float32)
    return (values * row_scale[:, None, None]).astype(jnp.bfloat16)


def draw_pairs(key, part):
    key = jax.random.fold_in(key, 5)
    group_count = TBLOCKS // TBLK_DEV
    slot_total = TBLK_DEV * QBLOCKS

    def one_group(group_pos):
        shuffled = jax.random.permutation(jax.random.fold_in(key, group_pos), slot_total - 2) + 1
        fixed_slots = jnp.array([0, slot_total - 1], dtype=jnp.int32)
        picked_slots = jnp.concatenate([fixed_slots, shuffled[:PAIRS_GROUP - 2].astype(jnp.int32)])
        return jnp.stack([picked_slots // QBLOCKS + group_pos * TBLK_DEV, picked_slots % QBLOCKS], axis=1)
    return jax.vmap(one_group)(jnp.arange(group_count, dtype=jnp.int32)).reshape(NPAIRS, 2).astype(jnp.int32)


def draw_counts(key, part):
    key = jax.random.fold_in(key, 11)
    base_counts = jax.random.randint(jax.random.fold_in(key, 1), (TBLOCKS,), max(1, TB // 4), TB + 1)
    chosen_slot = jax.random.randint(jax.random.fold_in(key, 2), (TBLOCKS // TBLK_DEV, 1), 0, TBLK_DEV)
    slot_pos = jnp.arange(TBLK_DEV, dtype=jnp.int32)[None, :]
    full_block = (slot_pos == chosen_slot).reshape(TBLOCKS)
    return jnp.where(full_block, TB, base_counts).astype(jnp.int32)


def shard_levels(rng, shape, pieces, low, high):
    gain = 1.0
    for dim, blocks in pieces:
        heights = jax.random.uniform(jax.random.fold_in(jax.random.fold_in(rng, 6), dim), (blocks,), jnp.float32, low / len(pieces), high / len(pieces))
        gain = gain * jnp.repeat(jnp.exp(heights), shape[dim] // blocks).reshape((-1,) + (1,) * (len(shape) - 1 - dim))
    return gain


def noise(key, shape, deviation, most, shards=(), held_as=jnp.bfloat16):
    drawn = jax.random.normal(key, shape, jnp.float32) * deviation
    if len(shards) > 0:
        drawn = shard_levels(key, shape, shards, -0.22, 0.18) * drawn
    return jnp.clip(drawn, min=-most, max=most).astype(held_as)


def setup_inputs(seed: int = 0) -> dict:
    streams_of = jax.random.split(jax.random.key(seed), 6)
    train_grad = noise(streams_of[0], (TRAIN, LAYERS, F), 1.0, 6.0, ((0, 8), (1, 4)))
    query_grad = noise(streams_of[1], (QBLOCKS, QB, LAYERS, F), (LAYERS * F) ** -0.5, 0.046875, ((0, 4), (2, 4)))
    sketch = draw_sketch(jax.random.fold_in(streams_of[5], 71), 0)
    pairs = draw_pairs(jax.random.fold_in(streams_of[5], 71), 0)
    counts = draw_counts(jax.random.fold_in(streams_of[5], 71), 0)
    return dict(train_grad=train_grad, query_grad=query_grad, sketch=sketch, pairs=pairs, counts=counts)


damp_ratio = 0.1

def precondition(sketch_layer, query_layer, damping):
    gram_matrix = jnp.dot(sketch_layer.astype(jnp.float32), sketch_layer.T.astype(jnp.float32), preferred_element_type=jnp.float32)
    factor = jnp.linalg.cholesky(gram_matrix + damping * jnp.eye(K, dtype=jnp.float32))
    projected = jnp.dot(sketch_layer.astype(jnp.float32), query_layer.T.astype(jnp.float32), preferred_element_type=jnp.float32)
    solved = jax.scipy.linalg.cho_solve((factor, True), projected)
    correction = jnp.dot(solved.astype(jnp.bfloat16).T.astype(jnp.float32), sketch_layer.astype(jnp.float32), preferred_element_type=jnp.float32)
    return ((query_layer.astype(jnp.float32) - correction) / damping).astype(jnp.bfloat16)

def reference(train_grad, query_grad, sketch, pairs, counts):
    energy = jnp.sum(jnp.square(sketch.astype(jnp.float32)))
    damping = damp_ratio * energy / (LAYERS * F)
    queries = query_grad.reshape(NQ, LAYERS, F)

    def layer_step(layer_pair):
        return precondition(layer_pair[0], layer_pair[1], damping)
    ready = lax.map(layer_step, (jnp.swapaxes(sketch, 0, 1), jnp.swapaxes(queries, 0, 1)))
    ready = jnp.swapaxes(ready, 0, 1).reshape(QBLOCKS, QB, LAYERS * F)
    train_blocks = train_grad.reshape(TBLOCKS, TB, LAYERS * F)

    def tile_of(pair_row):
        left_block = lax.dynamic_index_in_dim(train_blocks, pair_row[0], 0, keepdims=False)
        right_block = lax.dynamic_index_in_dim(ready, pair_row[1], 0, keepdims=False)
        product = jnp.dot(left_block.astype(jnp.float32), right_block.T.astype(jnp.float32), preferred_element_type=jnp.float32)
        limit = lax.dynamic_index_in_dim(counts, pair_row[0], 0, keepdims=False)
        keep_rows = jnp.arange(TB, dtype=jnp.int32)[:, None] < limit
        return jnp.where(keep_rows, product, jnp.zeros_like(product))
    return lax.map(tile_of, pairs)
```

```python
import functools

import jax
import jax.numpy as jnp
from jax import lax
from jax.experimental import pallas as pl
from jax.experimental.pallas import tpu as pltpu
from jax.sharding import PartitionSpec as P

damp_ratio = 0.1
TILE = 128
VMEM_BYTES = 56 * 1024 * 1024
NT = (((1,), (1,)), ((), ()))


def whole():
    return pl.BlockSpec(memory_space=pltpu.VMEM)


def in_smem():
    return pl.BlockSpec(memory_space=pltpu.SMEM)


def params():
    return pltpu.CompilerParams(vmem_limit_bytes=VMEM_BYTES)


def cost(flops, nbytes):
    return pl.CostEstimate(flops=flops, bytes_accessed=nbytes, transcendentals=0)


def invert_tile(a):
    n = a.shape[0]
    lane = lax.broadcasted_iota(jnp.int32, (n, n), 1)
    sub = lax.broadcasted_iota(jnp.int32, (n, n), 0)
    row_lane = lane[:1]
    for k in range(0, n, 4):
        col = [jnp.broadcast_to(a[:, k + i : k + i + 1], (n, n)) for i in range(4)]
        row = [a[k + i : k + i + 1, :] for i in range(4)]

        def entry(i, j):
            return jnp.broadcast_to(a[k + i : k + i + 1, k + j : k + j + 1], (1, n))

        p00, p01, p11 = entry(0, 0), entry(0, 1), entry(1, 1)
        q00, q01, q10, q11 = entry(2, 0), entry(2, 1), entry(3, 0), entry(3, 1)
        r00, r01, r11 = entry(2, 2), entry(2, 3), entry(3, 3)
        det = 1.0 / (p00 * p11 - p01 * p01)
        u00, u01, u11 = p11 * det, -p01 * det, p00 * det
        t00, t01 = q00 * u00 + q01 * u01, q00 * u01 + q01 * u11
        t10, t11 = q10 * u00 + q11 * u01, q10 * u01 + q11 * u11
        s00 = r00 - (t00 * q00 + t01 * q01)
        s01 = r01 - (t00 * q10 + t01 * q11)
        s11 = r11 - (t10 * q10 + t11 * q11)
        det = 1.0 / (s00 * s11 - s01 * s01)
        v00, v01, v11 = s11 * det, -s01 * det, s00 * det
        w00, w01 = v00 * t00 + v01 * t10, v00 * t01 + v01 * t11
        w10, w11 = v01 * t00 + v11 * t10, v01 * t01 + v11 * t11
        g00 = u00 + t00 * w00 + t10 * w10
        g01 = u01 + t00 * w01 + t10 * w11
        g11 = u11 + t01 * w01 + t11 * w11
        inv = [
            [g00, g01, -w00, -w10],
            [g01, g11, -w01, -w11],
            [-w00, -w01, v00, v01],
            [-w10, -w11, v01, v11],
        ]
        in_lane = (row_lane >= k) & (row_lane < k + 4)
        in_sub = (sub >= k) & (sub < k + 4)
        unit = [
            jnp.where(in_lane, jnp.where(row_lane == k + i, 1.0, 0.0), row[i]) for i in range(4)
        ]
        scaled = [
            inv[i][0] * unit[0] + inv[i][1] * unit[1] + inv[i][2] * unit[2] + inv[i][3] * unit[3]
            for i in range(4)
        ]
        left = [jnp.where(in_sub, jnp.where(sub == k + i, -1.0, 0.0), col[i]) for i in range(4)]
        a = jnp.where(((lane >= k) & (lane < k + 4)) | in_sub, 0.0, a)
        a = a - left[0] * scaled[0] - left[1] * scaled[1] - left[2] * scaled[2] - left[3] * scaled[3]
    return a


def full_dot(x, y):
    return jnp.dot(x, y, preferred_element_type=jnp.float32, precision=lax.Precision.HIGHEST)


def inverse_kernel(ratio, gram_ref, e0, e1, e2, e3, hi_ref, mid_ref, lo_ref, work):
    n = gram_ref.shape[0]
    energy = (e0[...] + e1[...] + e2[...] + e3[...])[:1, :1]
    diag = lax.broadcasted_iota(jnp.int32, (n, n), 0) == lax.broadcasted_iota(jnp.int32, (n, n), 1)
    work[...] = gram_ref[...] * (1.0 / energy) + jnp.where(diag, ratio, 0.0)
    for k in range(0, n, TILE):
        part = slice(k, k + TILE)
        tile_inv = invert_tile(work[part, part])
        col = work[:, part]
        row_new = full_dot(tile_inv, work[part, :])
        col_new = full_dot(col, tile_inv)
        work[...] = work[...] - full_dot(col, row_new)
        work[part, :] = row_new
        work[:, part] = col_new
        work[part, part] = -tile_inv
    x = -work[...]
    hi = x.astype(jnp.bfloat16)
    hi_ref[...] = hi
    x = x - hi.astype(jnp.float32)
    mid = x.astype(jnp.bfloat16)
    mid_ref[...] = mid
    lo_ref[...] = (x - mid.astype(jnp.float32)).astype(jnp.bfloat16)


def invert(gram, energies, ratio):
    n = gram.shape[0]
    return pl.pallas_call(
        functools.partial(inverse_kernel, ratio),
        out_shape=[jax.ShapeDtypeStruct((n, n), jnp.bfloat16)] * 3,
        in_specs=[whole()] * 5,
        out_specs=[whole()] * 3,
        scratch_shapes=[pltpu.VMEM((n, n), jnp.float32)],
        compiler_params=params(),
        cost_estimate=cost(20_000_000_000, 3_000_000),
        name="invert",
    )(gram, *energies)


def cross_kernel(where_ref, t_ref, q_ref, o0, o1, o2, o3, acc):
    parts = 4
    groups, _, rows, width = acc.shape
    prod = lax.dot_general(t_ref[...], q_ref[...], NT, preferred_element_type=jnp.float32)
    acc[...] = prod.reshape(groups, parts, rows, width)
    own = where_ref[1]
    for j, out in enumerate((o0, o1, o2, o3)):
        part = lax.rem(own + j, parts)
        out[...] = acc[:, part].astype(out.dtype)


def cross(where, train, queries):
    rows, depth = train.shape
    width = queries.shape[0]
    step = 512
    groups = step // TILE
    kept = TILE // 4
    out = (rows // TILE, kept, width)
    return pl.pallas_call(
        cross_kernel,
        grid=(rows // step,),
        in_specs=[
            in_smem(),
            pl.BlockSpec((step, depth), lambda i: (i, 0)),
            pl.BlockSpec((width, depth), lambda i: (0, 0)),
        ],
        out_specs=[pl.BlockSpec((groups, kept, width), lambda i: (i, 0, 0))] * 4,
        out_shape=[jax.ShapeDtypeStruct(out, jnp.float32)]
        + [jax.ShapeDtypeStruct(out, jnp.bfloat16)] * 3,
        scratch_shapes=[pltpu.VMEM((groups, 4, kept, width), jnp.float32)],
        compiler_params=params(),
        cost_estimate=cost(2 * rows * depth * width, 2 * (rows + width) * depth),
        name="cross",
    )(where, train, queries)


def tiles_kernel(
    where_ref, pairs_ref, e0, e1, e2, e3, c_ref, hi, mid, lo, p0, p1, p2, p3,
    o0, o1, o2, o3, solved, proj, tile,
):
    energy = (e0[...] + e1[...] + e2[...] + e3[...])[:1, :1]
    scale = 1.0 / energy
    step = 512
    for r in range(0, c_ref.shape[0], step):
        left = c_ref[r : r + step, :]
        prod = jnp.dot(left, lo[...], preferred_element_type=jnp.float32)
        prod += jnp.dot(left, mid[...], preferred_element_type=jnp.float32)
        prod += jnp.dot(left, hi[...], preferred_element_type=jnp.float32)
        solved[r : r + step, :] = (prod * scale).astype(jnp.bfloat16)
    for i, p in enumerate((p0, p1, p2, p3)):
        proj[i] = p[...]
    first = where_ref[0]
    own_layer = where_ref[1]
    own_query = where_ref[2]
    unroll = tile.shape[0]

    @pl.loop(0, pairs_ref.shape[0] // unroll)
    def _(g):
        for u in range(unroll):
            i = g * unroll + u
            block = pairs_ref[i, 0] - first
            query = pairs_ref[i, 1]
            source = lax.rem(own_query - lax.div(query, 4) + 4, 4)
            left = solved[pl.ds(pl.multiple_of(block * TILE, TILE), TILE), :]
            right = proj[source, pl.ds(pl.multiple_of(lax.rem(query, 4) * TILE, TILE), TILE), :]
            prod = lax.dot_general(left, right, NT, preferred_element_type=jnp.float32)
            tile[u] = prod.reshape(4, TILE // 4, TILE)
            for j, out in enumerate((o0, o1, o2, o3)):
                out[i] = tile[u, lax.rem(own_layer + j, 4)].astype(out.dtype)


def pair_tiles(where, pairs, energies, crossed, inverse, projections):
    count = pairs.shape[0]
    out = (count, TILE // 4, TILE)
    width = crossed.shape[1]
    return pl.pallas_call(
        tiles_kernel,
        in_specs=[in_smem(), in_smem()] + [whole()] * 12,
        out_specs=[whole()] * 4,
        out_shape=[jax.ShapeDtypeStruct(out, jnp.float32)]
        + [jax.ShapeDtypeStruct(out, jnp.bfloat16)] * 3,
        scratch_shapes=[
            pltpu.VMEM(crossed.shape, jnp.bfloat16),
            pltpu.VMEM((4, *projections[0].shape), jnp.bfloat16),
            pltpu.VMEM((4, 4, TILE // 4, TILE), jnp.float32),
        ],
        compiler_params=params(),
        cost_estimate=cost(6 * crossed.shape[0] * width * width, 8_000_000),
        name="pair_tiles",
    )(where, pairs, *energies, crossed, *inverse, *projections)


def finish_kernel(
    ratio, where_ref, pairs_ref, counts_ref, e0, e1, e2, e3, c0, c1, c2, c3, g0, g1, g2, g3,
    out_ref, store,
):
    energy = (e0[...] + e1[...] + e2[...] + e3[...])[:1, :1]
    damping = ratio * energy
    for i, g in enumerate((g0, g1, g2, g3)):
        store[i] = g[...].astype(jnp.float32)
    first = where_ref[0]
    own_layer = where_ref[1]
    own_query = where_ref[2]
    rows = out_ref.shape[1]
    row = lax.broadcasted_iota(jnp.int32, out_ref.shape[1:], 0) + own_layer * rows

    @pl.loop(0, pairs_ref.shape[0])
    def _(i):
        block = pairs_ref[i, 0] - first
        query = pairs_ref[i, 1]
        source = lax.rem(own_query - lax.div(query, 4) + 4, 4)
        column = pl.multiple_of(lax.rem(query, 4) * TILE, TILE)
        plain = store[source, block, :, pl.ds(column, TILE)]
        fix = c0[i] + c1[i].astype(jnp.float32) + c2[i].astype(jnp.float32)
        fix += c3[i].astype(jnp.float32)
        out_ref[i] = jnp.where(row < counts_ref[block], (plain - fix) / damping, 0.0)


def finish(where, pairs, counts, energies, fixes, plains, ratio):
    count = pairs.shape[0]
    return pl.pallas_call(
        functools.partial(finish_kernel, ratio),
        in_specs=[in_smem()] * 3 + [whole()] * 12,
        out_specs=whole(),
        out_shape=jax.ShapeDtypeStruct((count, TILE // 4, TILE), jnp.float32),
        scratch_shapes=[pltpu.VMEM((4, *plains[0].shape), jnp.float32)],
        compiler_params=params(),
        cost_estimate=cost(10_000_000, 8_000_000),
        name="finish",
    )(where, pairs, counts, *energies, *fixes, *plains)


def ring(n, d):
    return [(i, (i + d) % n) for i in range(n)]


def chip_ring(d):
    return [(i, (i // 2 + d) % 4 * 2 + i % 2) for i in range(8)]


OTHER_CORE = [(i, i ^ 1) for i in range(8)]


def local(train_grad, query_grad, sketch, pairs, counts):
    layer_count = lax.axis_size("layer")
    feature_count = sketch.shape[2]
    ratio = damp_ratio / (layer_count * feature_count)
    first = lax.axis_index("dp") * counts.shape[0]
    where = jnp.stack([first, lax.axis_index("layer"), lax.axis_index("query")]).astype(jnp.int32)
    train = train_grad.reshape(-1, feature_count)
    queries = query_grad.reshape(-1, feature_count)
    own = sketch.reshape(-1, feature_count)

    half = own.shape[0] // 2
    below = lax.ppermute(own, "dp", chip_ring(1))
    above = lax.ppermute(own, "dp", chip_ring(3))
    far_low = lax.ppermute(below[:half], "dp", chip_ring(1))
    far_high = lax.ppermute(above[half:], "dp", chip_ring(3))
    near = jnp.concatenate([own, below, above], axis=0)
    far = jnp.concatenate([far_low, far_high], axis=0)
    near_other = lax.ppermute(near, "dp", OTHER_CORE)
    far_other = lax.ppermute(far, "dp", OTHER_CORE)
    rows = jnp.concatenate([near, near_other, far, far_other], axis=0)

    kept, *sent = cross(where, train, queries)
    plain = kept
    for d, part in zip((1, 2, 3), sent):
        plain = plain + lax.ppermute(part, "layer", ring(4, d)).astype(jnp.float32)
    plain_sent = plain.astype(jnp.bfloat16)
    plains = [plain] + [lax.ppermute(plain_sent, "query", ring(4, d)) for d in (1, 2, 3)]

    gram = lax.dot_general(rows, rows, NT, preferred_element_type=jnp.float32)
    diag = jnp.eye(gram.shape[0], dtype=bool)
    energy = jnp.full((8, 128), jnp.sum(jnp.where(diag, gram, 0.0)), jnp.float32)
    energies = [energy] + [lax.ppermute(energy, "layer", ring(4, d)) for d in (1, 2, 3)]
    projected = lax.dot_general(queries, rows, NT, preferred_element_type=jnp.float32).astype(
        jnp.bfloat16
    )
    projections = [projected] + [lax.ppermute(projected, "query", ring(4, d)) for d in (1, 2, 3)]
    crossed = lax.dot_general(train, rows, NT, preferred_element_type=jnp.float32).astype(
        jnp.bfloat16
    )
    inverse = invert(gram, energies, ratio)
    fix, *fix_sent = pair_tiles(where, pairs, energies, crossed, inverse, projections)
    fixes = [fix] + [lax.ppermute(f, "layer", ring(4, d)) for d, f in zip((1, 2, 3), fix_sent)]
    return finish(where, pairs, counts, energies, fixes, plains, ratio)


def solution(mesh):
    placed = (
        P("dp", "layer", None),
        P("query", None, "layer", None),
        P("dp", "layer", None),
        P(("dp", "query"), None),
        P("dp"),
    )
    return jax.shard_map(
        local,
        mesh=mesh,
        in_specs=placed,
        out_specs=P(("dp", "query"), "layer", None),
        check_vma=False,
    )
```

```python
import functools

import jax
import jax.numpy as jnp
from jax import lax
from jax.experimental import pallas as pl
from jax.experimental.pallas import tpu as pltpu
from jax.sharding import PartitionSpec as P

damp_ratio = 0.1
TILE = 128
VMEM_BYTES = 56 * 1024 * 1024
NT = (((1,), (1,)), ((), ()))


def whole():
    return pl.BlockSpec(memory_space=pltpu.VMEM)


def in_smem():
    return pl.BlockSpec(memory_space=pltpu.SMEM)


def params():
    return pltpu.CompilerParams(vmem_limit_bytes=VMEM_BYTES)


def cost(flops, nbytes):
    return pl.CostEstimate(flops=flops, bytes_accessed=nbytes, transcendentals=0)


def invert_tile(a, beside):
    n = a.shape[0]
    lane = lax.broadcasted_iota(jnp.int32, (n, n), 1)
    sub = lax.broadcasted_iota(jnp.int32, (n, n), 0)
    row_lane = lane[:1]
    for k in range(0, n, 4):
        beside(k // 4)
        col = [jnp.broadcast_to(a[:, k + i : k + i + 1], (n, n)) for i in range(4)]
        row = [a[k + i : k + i + 1, :] for i in range(4)]

        def entry(i, j):
            return jnp.broadcast_to(a[k + i : k + i + 1, k + j : k + j + 1], (1, n))

        p00, p01, p11 = entry(0, 0), entry(0, 1), entry(1, 1)
        q00, q01, q10, q11 = entry(2, 0), entry(2, 1), entry(3, 0), entry(3, 1)
        r00, r01, r11 = entry(2, 2), entry(2, 3), entry(3, 3)
        det = 1.0 / (p00 * p11 - p01 * p01)
        u00, u01, u11 = p11 * det, -p01 * det, p00 * det
        t00, t01 = q00 * u00 + q01 * u01, q00 * u01 + q01 * u11
        t10, t11 = q10 * u00 + q11 * u01, q10 * u01 + q11 * u11
        s00 = r00 - (t00 * q00 + t01 * q01)
        s01 = r01 - (t00 * q10 + t01 * q11)
        s11 = r11 - (t10 * q10 + t11 * q11)
        det = 1.0 / (s00 * s11 - s01 * s01)
        v00, v01, v11 = s11 * det, -s01 * det, s00 * det
        w00, w01 = v00 * t00 + v01 * t10, v00 * t01 + v01 * t11
        w10, w11 = v01 * t00 + v11 * t10, v01 * t01 + v11 * t11
        g00 = u00 + t00 * w00 + t10 * w10
        g01 = u01 + t00 * w01 + t10 * w11
        g11 = u11 + t01 * w01 + t11 * w11
        inv = [
            [g00, g01, -w00, -w10],
            [g01, g11, -w01, -w11],
            [-w00, -w01, v00, v01],
            [-w10, -w11, v01, v11],
        ]
        in_lane = (row_lane >= k) & (row_lane < k + 4)
        in_sub = (sub >= k) & (sub < k + 4)
        unit = [
            jnp.where(in_lane, jnp.where(row_lane == k + i, 1.0, 0.0), row[i]) for i in range(4)
        ]
        scaled = [
            inv[i][0] * unit[0] + inv[i][1] * unit[1] + inv[i][2] * unit[2] + inv[i][3] * unit[3]
            for i in range(4)
        ]
        left = [jnp.where(in_sub, jnp.where(sub == k + i, -1.0, 0.0), col[i]) for i in range(4)]
        a = jnp.where(((lane >= k) & (lane < k + 4)) | in_sub, 0.0, a)
        a = a - left[0] * scaled[0] - left[1] * scaled[1] - left[2] * scaled[2] - left[3] * scaled[3]
    return a


def full_dot(x, y):
    return jnp.dot(x, y, preferred_element_type=jnp.float32, precision=lax.Precision.HIGHEST)


def solve_kernel(
    ratio, gram_ref, e0, e1, e2, e3, rows_ref, train_hbm, out_ref, train_ref, cross_ref, train_sems
):
    n = gram_ref.shape[0]
    blocks = n // TILE
    step = train_ref.shape[0] // blocks
    train_copies = [
        pltpu.make_async_copy(
            train_hbm.at[pl.ds(r * step, step), :],
            train_ref.at[pl.ds(r * step, step), :],
            train_sems.at[r],
        )
        for r in range(blocks)
    ]
    for copy in train_copies:
        copy.start()
    energy = (e0[...] + e1[...] + e2[...] + e3[...])[:1, :1]
    scale = 1.0 / energy
    diag = lax.broadcasted_iota(jnp.int32, (n, n), 0) == lax.broadcasted_iota(jnp.int32, (n, n), 1)
    full = gram_ref[...] * scale + jnp.where(diag, ratio, 0.0)
    slabs = [full[i * TILE : (i + 1) * TILE] for i in range(blocks)]
    lane_block = lax.broadcasted_iota(jnp.int32, (TILE, n), 1) // TILE
    chunk = rows_ref.shape[1] // 16

    for k in range(blocks):
        part = slice(k * TILE, (k + 1) * TILE)
        held = slice(k * step, (k + 1) * step)
        train_copies[k].wait()

        def beside(s, k=k, held=held):
            if s % 2:
                return
            piece = s // 2
            depth = slice(piece * chunk, (piece + 1) * chunk)
            prod = lax.dot_general(
                train_ref[held, depth], rows_ref[:, depth], NT, preferred_element_type=jnp.float32
            )
            if piece == 0:
                cross_ref[held, :] = prod
            else:
                cross_ref[held, :] += prod

        tile_inv = invert_tile(slabs[k][:, part], beside)
        new = full_dot(tile_inv, jnp.where(lane_block == k, 0.0, slabs[k]))
        new = jnp.concatenate(
            [tile_inv if j == k else new[:, j * TILE : (j + 1) * TILE] for j in range(blocks)],
            axis=1,
        )
        for d in range(1, blocks):
            i = (k + d) % blocks
            slabs[i] = jnp.where(lane_block == k, 0.0, slabs[i]) - full_dot(slabs[i][:, part], new)
        slabs[k] = new
    x = jnp.concatenate(slabs, axis=0)
    hi = x.astype(jnp.bfloat16)
    x = x - hi.astype(jnp.float32)
    mid = x.astype(jnp.bfloat16)
    lo = (x - mid.astype(jnp.float32)).astype(jnp.bfloat16)
    for k in range(blocks):
        held = slice(k * step, (k + 1) * step)
        left = cross_ref[held, :]
        left_hi = left.astype(jnp.bfloat16)
        left_lo = (left - left_hi.astype(jnp.float32)).astype(jnp.bfloat16)
        prod = jnp.dot(left_hi, lo, preferred_element_type=jnp.float32)
        prod += jnp.dot(left_hi, mid, preferred_element_type=jnp.float32)
        prod += jnp.dot(left_lo, hi, preferred_element_type=jnp.float32)
        prod += jnp.dot(left_hi, hi, preferred_element_type=jnp.float32)
        out_ref[held, :] = (prod * scale).astype(jnp.bfloat16)


def solve(gram, energies, sketch_rows, train, ratio):
    n = gram.shape[0]
    rows, depth = train.shape
    return pl.pallas_call(
        functools.partial(solve_kernel, ratio),
        out_shape=jax.ShapeDtypeStruct((rows, n), jnp.bfloat16),
        in_specs=[whole()] * 6 + [pl.BlockSpec(memory_space=pl.ANY)],
        out_specs=whole(),
        scratch_shapes=[
            pltpu.VMEM((rows, depth), jnp.bfloat16),
            pltpu.VMEM((rows, n), jnp.float32),
            pltpu.SemaphoreType.DMA((n // TILE,)),
        ],
        compiler_params=params(),
        cost_estimate=cost(40_000_000_000, 30_000_000),
        name="solve",
    )(gram, *energies, sketch_rows, train)


def cross_kernel(given, where_ref, t_ref, q_ref, *refs):
    o0, o1, o2, o3, acc = refs[given:]
    groups, parts, rows, width = acc.shape
    prod = lax.dot_general(t_ref[...], q_ref[...], NT, preferred_element_type=jnp.float32)
    acc[...] = prod.reshape(groups, parts, rows, width)
    own = where_ref[1]
    for j, out in enumerate((o0, o1, o2, o3)):
        part = lax.rem(own + j, parts)
        out[...] = acc[:, part].astype(out.dtype)


def cross(where, train, queries, half, filled=()):
    rows, depth = train.shape
    width = queries.shape[0]
    step = 512
    steps = rows // step // 2
    groups = step // TILE
    kept = TILE // 4
    out = (rows // TILE, kept, width)
    start = half * steps
    return pl.pallas_call(
        functools.partial(cross_kernel, len(filled)),
        grid=(steps,),
        in_specs=[
            in_smem(),
            pl.BlockSpec((step, depth), lambda i: (start + i, 0)),
            pl.BlockSpec((width, depth), lambda i: (0, 0)),
        ]
        + [pl.BlockSpec(memory_space=pl.ANY)] * len(filled),
        out_specs=[pl.BlockSpec((groups, kept, width), lambda i: (start + i, 0, 0))] * 4,
        out_shape=[jax.ShapeDtypeStruct(out, jnp.float32)]
        + [jax.ShapeDtypeStruct(out, jnp.bfloat16)] * 3,
        scratch_shapes=[pltpu.VMEM((groups, 4, kept, width), jnp.float32)],
        input_output_aliases={3 + j: j for j in range(len(filled))},
        compiler_params=params(),
        cost_estimate=cost(rows * depth * width, 2 * (rows + width) * depth),
        name="cross",
    )(where, train, queries, *filled)


def dots_kernel(*refs):
    *pieces, q_ref, rows_ref, gram_ref, energy_ref, proj_ref, sums = refs
    k = pl.program_id(0)
    start = 0
    for piece in pieces:
        rows_ref[start : start + piece.shape[0], :] = piece[...]
        start += piece.shape[0]
    n = gram_ref.shape[0]
    rows = rows_ref[...]
    for part, left in ((slice(0, n), rows), (slice(n, None), q_ref[...])):
        prod = lax.dot_general(left, rows, NT, preferred_element_type=jnp.float32)
        sums[part, :] = jnp.where(k == 0, 0.0, sums[part, :]) + prod

    @pl.when(k == pl.num_programs(0) - 1)
    def _():
        gram = sums[:n, :]
        gram_ref[...] = gram
        proj_ref[...] = sums[n:, :].astype(jnp.bfloat16)
        diag = lax.broadcasted_iota(jnp.int32, (n, n), 0) == lax.broadcasted_iota(
            jnp.int32, (n, n), 1
        )
        trace = jnp.sum(jnp.where(diag, gram, 0.0))
        energy_ref[...] = jnp.full(energy_ref.shape, trace, jnp.float32)


def dots(pieces, queries):
    n = sum(piece.shape[0] for piece in pieces)
    width, depth = queries.shape
    chunk = 1024
    return pl.pallas_call(
        dots_kernel,
        grid=(depth // chunk,),
        in_specs=[
            pl.BlockSpec((piece.shape[0], chunk), lambda k: (0, k)) for piece in (*pieces, queries)
        ],
        out_specs=[pl.BlockSpec((n, chunk), lambda k: (0, k))] + [whole()] * 3,
        out_shape=[
            jax.ShapeDtypeStruct((n, depth), jnp.bfloat16),
            jax.ShapeDtypeStruct((n, n), jnp.float32),
            jax.ShapeDtypeStruct((8, 128), jnp.float32),
            jax.ShapeDtypeStruct((width, n), jnp.bfloat16),
        ],
        scratch_shapes=[pltpu.VMEM((n + width, n), jnp.float32)],
        compiler_params=params(),
        cost_estimate=cost(2 * n * depth * (n + width), 12_000_000),
        name="dots",
    )(*pieces, queries)


def tiles_kernel(
    ratio, where_ref, pairs_ref, counts_ref, e0, e1, e2, e3, solved, p0, p1, p2, p3,
    o0, o1, o2, o3, proj, tile,
):
    energy = (e0[...] + e1[...] + e2[...] + e3[...])[:1, :1]
    scale = 1.0 / (ratio * energy)
    for i, p in enumerate((p0, p1, p2, p3)):
        proj[i] = p[...].reshape(proj.shape[1:])
    first = where_ref[0]
    own_layer = where_ref[1]
    own_query = where_ref[2]
    unroll = tile.shape[0]
    row = lax.broadcasted_iota(jnp.int32, (TILE, TILE), 0)

    @pl.loop(0, pairs_ref.shape[0] // unroll)
    def _(g):
        for u in range(unroll):
            i = g * unroll + u
            block = pairs_ref[i, 0] - first
            query = pairs_ref[i, 1]
            source = lax.rem(own_query - lax.div(query, 4) + 4, 4)
            left = solved[pl.ds(pl.multiple_of(block * TILE, TILE), TILE), :]
            right = proj[source, lax.rem(query, 4)]
            prod = lax.dot_general(left, right, NT, preferred_element_type=jnp.float32) * scale
            prod = jnp.where(row < counts_ref[block], prod, 0.0)
            tile[u] = prod.reshape(4, TILE // 4, TILE)
        for u in range(unroll):
            i = g * unroll + u
            for j, out in enumerate((o0, o1, o2, o3)):
                out[i] = tile[u, lax.rem(own_layer + j, 4)].astype(out.dtype)


def pair_tiles(where, pairs, counts, energies, solved, projections, ratio):
    count = pairs.shape[0]
    out = (count, TILE // 4, TILE)
    depth = solved.shape[1]
    return pl.pallas_call(
        functools.partial(tiles_kernel, ratio),
        in_specs=[in_smem()] * 3 + [whole()] * 9,
        out_specs=[whole()] * 4,
        out_shape=[jax.ShapeDtypeStruct(out, jnp.float32)]
        + [jax.ShapeDtypeStruct(out, jnp.bfloat16)] * 3,
        scratch_shapes=[
            pltpu.VMEM((4, 4, TILE, depth), jnp.bfloat16),
            pltpu.VMEM((16, 4, TILE // 4, TILE), jnp.float32),
        ],
        compiler_params=params(),
        cost_estimate=cost(1000, 1000),
        name="pair_tiles",
    )(where, pairs, counts, *energies, solved, *projections)


def select_kernel(
    ratio, where_ref, pairs_ref, counts_ref, e0, e1, e2, e3, g0, g1, g3, low, high, out_ref
):
    energy = (e0[...] + e1[...] + e2[...] + e3[...])[:1, :1]
    scale = 1.0 / (ratio * energy)
    first = where_ref[0]
    own_layer = where_ref[1]
    own_query = where_ref[2]
    count, rows, _ = out_ref.shape
    row = lax.broadcasted_iota(jnp.int32, out_ref.shape[1:], 0) + own_layer * rows
    half = low.shape[0]
    unroll = 8

    @pl.loop(0, count // unroll)
    def _(g):
        for u in range(unroll):
            i = g * unroll + u
            block = pairs_ref[i, 0] - first
            query = pairs_ref[i, 1]
            source = lax.rem(own_query - lax.div(query, 4) + 4, 4)
            column = pl.ds(pl.multiple_of(lax.rem(query, 4) * TILE, TILE), TILE)
            plain = g0[block, :, column]
            far = jnp.where(
                block < half,
                low[jnp.minimum(block, half - 1), :, column],
                high[jnp.maximum(block - half, 0), :, column],
            )
            for d, part in ((1, g1[block, :, column]), (2, far), (3, g3[block, :, column])):
                plain = jnp.where(source == d, part.astype(jnp.float32), plain)
            out_ref[i] = jnp.where(row < counts_ref[block], plain * scale, 0.0)


def select(where, pairs, counts, energies, plains, ratio):
    count = pairs.shape[0]
    return pl.pallas_call(
        functools.partial(select_kernel, ratio),
        in_specs=[in_smem()] * 3 + [whole()] * 9,
        out_specs=whole(),
        out_shape=jax.ShapeDtypeStruct((count, TILE // 4, TILE), jnp.float32),
        compiler_params=params(),
        cost_estimate=cost(1000, 1000),
        name="select",
    )(where, pairs, counts, *energies, *plains)


def ring(n, d):
    return [(i, (i + d) % n) for i in range(n)]


def chip_ring(d):
    return [(i, (i // 2 + d) % 4 * 2 + i % 2) for i in range(8)]


OTHER_CORE = [(i, i ^ 1) for i in range(8)]


def local(train_grad, query_grad, sketch, pairs, counts):
    layer_count = lax.axis_size("layer")
    feature_count = sketch.shape[2]
    ratio = damp_ratio / (layer_count * feature_count)
    first = lax.axis_index("dp") * counts.shape[0]
    where = jnp.stack([first, lax.axis_index("layer"), lax.axis_index("query")]).astype(jnp.int32)
    train = train_grad.reshape(-1, feature_count)
    queries = query_grad.reshape(-1, feature_count)
    own = sketch.reshape(-1, feature_count)

    below = lax.ppermute(own, "dp", chip_ring(1))
    above = lax.ppermute(own, "dp", chip_ring(3))
    products = cross(where, train, queries, 0)
    below, above, products = lax.optimization_barrier((below, above, products))
    half = own.shape[0] // 2
    far = [
        lax.ppermute(below[:half], "dp", chip_ring(1)),
        lax.ppermute(above[half:], "dp", chip_ring(3)),
    ]
    products = cross(where, train, queries, 1, products)
    far, products = lax.optimization_barrier((far, products))
    kept, *sent = products
    pieces = [own, below, above, *far]
    pieces += [lax.ppermute(piece, "dp", OTHER_CORE) for piece in pieces]
    rows, gram, energy, projected = dots(pieces, queries)

    energies = [lax.ppermute(energy, "layer", ring(4, d)) for d in (1, 2, 3)]
    projections = [projected] + [lax.ppermute(projected, "query", ring(4, d)) for d in (1, 2, 3)]

    energies, sent = lax.optimization_barrier((energies, sent))
    energies = [energy, *energies]
    taken = [lax.ppermute(part, "layer", ring(4, d)) for d, part in zip((1, 2, 3), sent)]
    solved = solve(gram, energies, rows, train, ratio)

    taken, solved, projections = lax.optimization_barrier((taken, solved, projections))
    plain = kept
    for part in taken:
        plain = plain + part.astype(jnp.float32)
    plain_sent = plain.astype(jnp.bfloat16)
    before = lax.ppermute(plain_sent, "query", ring(4, 1))
    after = lax.ppermute(plain_sent, "query", ring(4, 3))
    solved, plain_sent = lax.optimization_barrier((solved, plain_sent))

    fix, *fix_sent = pair_tiles(where, pairs, counts, energies, solved, projections, ratio)
    fixes = [lax.ppermute(f, "layer", ring(4, d)) for d, f in zip((1, 2, 3), fix_sent)]
    before, after, fix = lax.optimization_barrier((before, after, fix))
    half = before.shape[0] // 2
    low = lax.ppermute(before[:half], "query", ring(4, 1))
    high = lax.ppermute(after[half:], "query", ring(4, 3))
    plains = [plain, before, after, low, high]
    result = select(where, pairs, counts, energies, plains, ratio)
    for part in fixes:
        fix = fix + part.astype(jnp.float32)
    return result - fix


def solution(mesh):
    placed = (
        P("dp", "layer", None),
        P("query", None, "layer", None),
        P("dp", "layer", None),
        P(("dp", "query"), None),
        P("dp"),
    )
    return jax.shard_map(
        local,
        mesh=mesh,
        in_specs=placed,
        out_specs=P(("dp", "query"), "layer", None),
        check_vma=False,
    )
```

```python
import functools

import jax
import jax.numpy as jnp
from jax import lax
from jax.experimental import pallas as pl
from jax.experimental.pallas import tpu as pltpu
from jax.sharding import PartitionSpec as P

damp_ratio = 0.1
TILE = 128
VMEM_BYTES = 56 * 1024 * 1024
NT = (((1,), (1,)), ((), ()))


def whole():
    return pl.BlockSpec(memory_space=pltpu.VMEM)


def in_smem():
    return pl.BlockSpec(memory_space=pltpu.SMEM)


def params():
    return pltpu.CompilerParams(vmem_limit_bytes=VMEM_BYTES)


def cost(flops, nbytes):
    return pl.CostEstimate(flops=flops, bytes_accessed=nbytes, transcendentals=0)


def invert_tile(a, beside):
    n = a.shape[0]
    lane = lax.broadcasted_iota(jnp.int32, (n, n), 1)
    sub = lax.broadcasted_iota(jnp.int32, (n, n), 0)
    row_lane = lane[:1]
    for k in range(0, n, 4):
        beside(k // 4)
        col = [jnp.broadcast_to(a[:, k + i : k + i + 1], (n, n)) for i in range(4)]
        row = [a[k + i : k + i + 1, :] for i in range(4)]

        def entry(i, j):
            return jnp.broadcast_to(a[k + i : k + i + 1, k + j : k + j + 1], (1, n))

        p00, p01, p11 = entry(0, 0), entry(0, 1), entry(1, 1)
        q00, q01, q10, q11 = entry(2, 0), entry(2, 1), entry(3, 0), entry(3, 1)
        r00, r01, r11 = entry(2, 2), entry(2, 3), entry(3, 3)
        det = 1.0 / (p00 * p11 - p01 * p01)
        u00, u01, u11 = p11 * det, -p01 * det, p00 * det
        t00, t01 = q00 * u00 + q01 * u01, q00 * u01 + q01 * u11
        t10, t11 = q10 * u00 + q11 * u01, q10 * u01 + q11 * u11
        s00 = r00 - (t00 * q00 + t01 * q01)
        s01 = r01 - (t00 * q10 + t01 * q11)
        s11 = r11 - (t10 * q10 + t11 * q11)
        det = 1.0 / (s00 * s11 - s01 * s01)
        v00, v01, v11 = s11 * det, -s01 * det, s00 * det
        w00, w01 = v00 * t00 + v01 * t10, v00 * t01 + v01 * t11
        w10, w11 = v01 * t00 + v11 * t10, v01 * t01 + v11 * t11
        g00 = u00 + t00 * w00 + t10 * w10
        g01 = u01 + t00 * w01 + t10 * w11
        g11 = u11 + t01 * w01 + t11 * w11
        inv = [
            [g00, g01, -w00, -w10],
            [g01, g11, -w01, -w11],
            [-w00, -w01, v00, v01],
            [-w10, -w11, v01, v11],
        ]
        in_lane = (row_lane >= k) & (row_lane < k + 4)
        in_sub = (sub >= k) & (sub < k + 4)
        unit = [
            jnp.where(in_lane, jnp.where(row_lane == k + i, 1.0, 0.0), row[i]) for i in range(4)
        ]
        scaled = [
            inv[i][0] * unit[0] + inv[i][1] * unit[1] + inv[i][2] * unit[2] + inv[i][3] * unit[3]
            for i in range(4)
        ]
        left = [jnp.where(in_sub, jnp.where(sub == k + i, -1.0, 0.0), col[i]) for i in range(4)]
        a = jnp.where(((lane >= k) & (lane < k + 4)) | in_sub, 0.0, a)
        a = a - left[0] * scaled[0] - left[1] * scaled[1] - left[2] * scaled[2] - left[3] * scaled[3]
    return a


def full_dot(x, y):
    return jnp.dot(x, y, preferred_element_type=jnp.float32, precision=lax.Precision.HIGHEST)


def solve_kernel(
    ratio, gram_ref, e0, e1, e2, e3, rows_ref, train_hbm, out_ref, train_ref, cross_ref, train_sems
):
    n = gram_ref.shape[0]
    blocks = n // TILE
    step = train_ref.shape[0] // blocks
    train_copies = [
        pltpu.make_async_copy(
            train_hbm.at[pl.ds(r * step, step), :],
            train_ref.at[pl.ds(r * step, step), :],
            train_sems.at[r],
        )
        for r in range(blocks)
    ]
    for copy in train_copies:
        copy.start()
    energy = (e0[...] + e1[...] + e2[...] + e3[...])[:1, :1]
    scale = 1.0 / energy
    diag = lax.broadcasted_iota(jnp.int32, (n, n), 0) == lax.broadcasted_iota(jnp.int32, (n, n), 1)
    full = gram_ref[...] * scale + jnp.where(diag, ratio, 0.0)
    slabs = [full[i * TILE : (i + 1) * TILE] for i in range(blocks)]
    lane_block = lax.broadcasted_iota(jnp.int32, (TILE, n), 1) // TILE
    chunk = rows_ref.shape[1] // 16

    for k in range(blocks):
        part = slice(k * TILE, (k + 1) * TILE)
        held = slice(k * step, (k + 1) * step)
        train_copies[k].wait()

        def beside(s, k=k, held=held):
            if s % 2:
                return
            piece = s // 2
            depth = slice(piece * chunk, (piece + 1) * chunk)
            prod = lax.dot_general(
                train_ref[held, depth], rows_ref[:, depth], NT, preferred_element_type=jnp.float32
            )
            if piece == 0:
                cross_ref[held, :] = prod
            else:
                cross_ref[held, :] += prod

        tile_inv = invert_tile(slabs[k][:, part], beside)
        new = full_dot(tile_inv, jnp.where(lane_block == k, 0.0, slabs[k]))
        new = jnp.concatenate(
            [tile_inv if j == k else new[:, j * TILE : (j + 1) * TILE] for j in range(blocks)],
            axis=1,
        )
        for d in range(1, blocks):
            i = (k + d) % blocks
            slabs[i] = jnp.where(lane_block == k, 0.0, slabs[i]) - full_dot(slabs[i][:, part], new)
        slabs[k] = new
    x = jnp.concatenate(slabs, axis=0)
    hi = x.astype(jnp.bfloat16)
    x = x - hi.astype(jnp.float32)
    mid = x.astype(jnp.bfloat16)
    lo = (x - mid.astype(jnp.float32)).astype(jnp.bfloat16)
    for k in range(blocks):
        held = slice(k * step, (k + 1) * step)
        left = cross_ref[held, :]
        left_hi = left.astype(jnp.bfloat16)
        left_lo = (left - left_hi.astype(jnp.float32)).astype(jnp.bfloat16)
        prod = jnp.dot(left_hi, lo, preferred_element_type=jnp.float32)
        prod += jnp.dot(left_hi, mid, preferred_element_type=jnp.float32)
        prod += jnp.dot(left_lo, hi, preferred_element_type=jnp.float32)
        prod += jnp.dot(left_hi, hi, preferred_element_type=jnp.float32)
        out_ref[held, :] = (prod * scale).astype(jnp.bfloat16)


def solve(gram, energies, sketch_rows, train, ratio):
    n = gram.shape[0]
    rows, depth = train.shape
    return pl.pallas_call(
        functools.partial(solve_kernel, ratio),
        out_shape=jax.ShapeDtypeStruct((rows, n), jnp.bfloat16),
        in_specs=[whole()] * 6 + [pl.BlockSpec(memory_space=pl.ANY)],
        out_specs=whole(),
        scratch_shapes=[
            pltpu.VMEM((rows, depth), jnp.bfloat16),
            pltpu.VMEM((rows, n), jnp.float32),
            pltpu.SemaphoreType.DMA((n // TILE,)),
        ],
        compiler_params=params(),
        cost_estimate=cost(40_000_000_000, 30_000_000),
        name="solve",
    )(gram, *energies, sketch_rows, train)


def cross_kernel(given, where_ref, t_ref, q_ref, *refs):
    o0, o1, o2, o3, acc = refs[given:]
    groups, parts, rows, width = acc.shape
    prod = lax.dot_general(t_ref[...], q_ref[...], NT, preferred_element_type=jnp.float32)
    acc[...] = prod.reshape(groups, parts, rows, width)
    own = where_ref[1]
    for j, out in enumerate((o0, o1, o2, o3)):
        part = lax.rem(own + j, parts)
        out[...] = acc[:, part].astype(out.dtype)


def cross(where, train, queries, start, steps, filled=()):
    rows, depth = train.shape
    width = queries.shape[0]
    step = 512
    groups = step // TILE
    kept = TILE // 4
    out = (rows // TILE, kept, width)
    return pl.pallas_call(
        functools.partial(cross_kernel, len(filled)),
        grid=(steps,),
        in_specs=[
            in_smem(),
            pl.BlockSpec((step, depth), lambda i: (start + i, 0)),
            pl.BlockSpec((width, depth), lambda i: (0, 0)),
        ]
        + [pl.BlockSpec(memory_space=pl.ANY)] * len(filled),
        out_specs=[pl.BlockSpec((groups, kept, width), lambda i: (start + i, 0, 0))] * 4,
        out_shape=[jax.ShapeDtypeStruct(out, jnp.float32)]
        + [jax.ShapeDtypeStruct(out, jnp.bfloat16)] * 3,
        scratch_shapes=[pltpu.VMEM((groups, 4, kept, width), jnp.float32)],
        input_output_aliases={3 + j: j for j in range(len(filled))},
        compiler_params=params(),
        cost_estimate=cost(2 * steps * step * depth * width, 2 * (steps * step + width) * depth),
        name="cross",
    )(where, train, queries, *filled)


def dots_kernel(*refs):
    *pieces, q_ref, rows_ref, gram_ref, energy_ref, proj_ref, sums = refs
    k = pl.program_id(0)
    start = 0
    for piece in pieces:
        rows_ref[start : start + piece.shape[0], :] = piece[...]
        start += piece.shape[0]
    n = gram_ref.shape[0]
    rows = rows_ref[...]
    for part, left in ((slice(0, n), rows), (slice(n, None), q_ref[...])):
        prod = lax.dot_general(left, rows, NT, preferred_element_type=jnp.float32)
        sums[part, :] = jnp.where(k == 0, 0.0, sums[part, :]) + prod

    @pl.when(k == pl.num_programs(0) - 1)
    def _():
        gram = sums[:n, :]
        gram_ref[...] = gram
        proj_ref[...] = sums[n:, :].astype(jnp.bfloat16)
        diag = lax.broadcasted_iota(jnp.int32, (n, n), 0) == lax.broadcasted_iota(
            jnp.int32, (n, n), 1
        )
        trace = jnp.sum(jnp.where(diag, gram, 0.0))
        energy_ref[...] = jnp.full(energy_ref.shape, trace, jnp.float32)


def dots(pieces, queries):
    n = sum(piece.shape[0] for piece in pieces)
    width, depth = queries.shape
    chunk = 2048
    return pl.pallas_call(
        dots_kernel,
        grid=(depth // chunk,),
        in_specs=[
            pl.BlockSpec((piece.shape[0], chunk), lambda k: (0, k)) for piece in (*pieces, queries)
        ],
        out_specs=[pl.BlockSpec((n, chunk), lambda k: (0, k))] + [whole()] * 3,
        out_shape=[
            jax.ShapeDtypeStruct((n, depth), jnp.bfloat16),
            jax.ShapeDtypeStruct((n, n), jnp.float32),
            jax.ShapeDtypeStruct((8, 128), jnp.float32),
            jax.ShapeDtypeStruct((width, n), jnp.bfloat16),
        ],
        scratch_shapes=[pltpu.VMEM((n + width, n), jnp.float32)],
        compiler_params=params(),
        cost_estimate=cost(2 * n * depth * (n + width), 12_000_000),
        name="dots",
    )(*pieces, queries)


def tiles_kernel(
    ratio, where_ref, pairs_ref, counts_ref, e0, e1, e2, e3, solved, p0, p1, p2, p3,
    o0, o1, o2, o3, proj, tile,
):
    energy = (e0[...] + e1[...] + e2[...] + e3[...])[:1, :1]
    scale = 1.0 / (ratio * energy)
    for i, p in enumerate((p0, p1, p2, p3)):
        proj[i] = p[...].reshape(proj.shape[1:])
    first = where_ref[0]
    own_layer = where_ref[1]
    own_query = where_ref[2]
    unroll = tile.shape[0]
    row = lax.broadcasted_iota(jnp.int32, (TILE, TILE), 0)

    @pl.loop(0, pairs_ref.shape[0] // unroll)
    def _(g):
        for u in range(unroll):
            i = g * unroll + u
            block = pairs_ref[i, 0] - first
            query = pairs_ref[i, 1]
            place = lax.div(query, 4)
            second = jnp.where(place + own_query == 3, 2, 3)
            first_or_second = jnp.where(place == jnp.bitwise_xor(own_query, 1), 1, second)
            source = jnp.where(place == own_query, 0, first_or_second)
            left = solved[pl.ds(pl.multiple_of(block * TILE, TILE), TILE), :]
            right = proj[source, lax.rem(query, 4)]
            prod = lax.dot_general(left, right, NT, preferred_element_type=jnp.float32) * scale
            prod = jnp.where(row < counts_ref[block], prod, 0.0)
            tile[u] = prod.reshape(4, TILE // 4, TILE)
        for u in range(unroll):
            i = g * unroll + u
            for j, out in enumerate((o0, o1, o2, o3)):
                out[i] = tile[u, lax.rem(own_layer + j, 4)].astype(out.dtype)


def pair_tiles(where, pairs, counts, energies, solved, projections, ratio):
    count = pairs.shape[0]
    out = (count, TILE // 4, TILE)
    depth = solved.shape[1]
    return pl.pallas_call(
        functools.partial(tiles_kernel, ratio),
        in_specs=[in_smem()] * 3 + [whole()] * 9,
        out_specs=[whole()] * 4,
        out_shape=[jax.ShapeDtypeStruct(out, jnp.float32)]
        + [jax.ShapeDtypeStruct(out, jnp.bfloat16)] * 3,
        scratch_shapes=[
            pltpu.VMEM((4, 4, TILE, depth), jnp.bfloat16),
            pltpu.VMEM((16, 4, TILE // 4, TILE), jnp.float32),
        ],
        compiler_params=params(),
        cost_estimate=cost(1000, 1000),
        name="pair_tiles",
    )(where, pairs, counts, *energies, solved, *projections)


def select_kernel(
    ratio, where_ref, pairs_ref, counts_ref, e0, e1, e2, e3, g0, g1, g3, low, high, out_ref
):
    energy = (e0[...] + e1[...] + e2[...] + e3[...])[:1, :1]
    scale = 1.0 / (ratio * energy)
    first = where_ref[0]
    own_layer = where_ref[1]
    own_query = where_ref[2]
    count, rows, _ = out_ref.shape
    row = lax.broadcasted_iota(jnp.int32, out_ref.shape[1:], 0) + own_layer * rows
    half = low.shape[0]
    unroll = 8

    @pl.loop(0, count // unroll)
    def _(g):
        for u in range(unroll):
            i = g * unroll + u
            block = pairs_ref[i, 0] - first
            query = pairs_ref[i, 1]
            source = lax.rem(own_query - lax.div(query, 4) + 4, 4)
            column = pl.ds(pl.multiple_of(lax.rem(query, 4) * TILE, TILE), TILE)
            plain = g0[block, :, column]
            far = jnp.where(
                block < half,
                low[jnp.minimum(block, half - 1), :, column],
                high[jnp.maximum(block - half, 0), :, column],
            )
            for d, part in ((1, g1[block, :, column]), (2, far), (3, g3[block, :, column])):
                plain = jnp.where(source == d, part.astype(jnp.float32), plain)
            out_ref[i] = jnp.where(row < counts_ref[block], plain * scale, 0.0)


def select(where, pairs, counts, energies, plains, ratio):
    count = pairs.shape[0]
    return pl.pallas_call(
        functools.partial(select_kernel, ratio),
        in_specs=[in_smem()] * 3 + [whole()] * 9,
        out_specs=whole(),
        out_shape=jax.ShapeDtypeStruct((count, TILE // 4, TILE), jnp.float32),
        compiler_params=params(),
        cost_estimate=cost(1000, 1000),
        name="select",
    )(where, pairs, counts, *energies, *plains)


def ring(n, d):
    return [(i, (i + d) % n) for i in range(n)]


def chip_ring(d):
    return [(i, (i // 2 + d) % 4 * 2 + i % 2) for i in range(8)]


OTHER_CORE = [(i, i ^ 1) for i in range(8)]
BESIDE = [(i, i ^ 1) for i in range(4)]
ACROSS = [(i, 3 - i) for i in range(4)]


def local(train_grad, query_grad, sketch, pairs, counts):
    layer_count = lax.axis_size("layer")
    feature_count = sketch.shape[2]
    ratio = damp_ratio / (layer_count * feature_count)
    first = lax.axis_index("dp") * counts.shape[0]
    where = jnp.stack([first, lax.axis_index("layer"), lax.axis_index("query")]).astype(jnp.int32)
    train = train_grad.reshape(-1, feature_count)
    queries = query_grad.reshape(-1, feature_count)
    own = sketch.reshape(-1, feature_count)

    below = lax.ppermute(own, "dp", chip_ring(1))
    above = lax.ppermute(own, "dp", chip_ring(3))
    products = cross(where, train, queries, 0, 3)
    below, above, products = lax.optimization_barrier((below, above, products))
    half = own.shape[0] // 2
    far = [
        lax.ppermute(below[:half], "dp", chip_ring(1)),
        lax.ppermute(above[half:], "dp", chip_ring(3)),
    ]
    products = cross(where, train, queries, 3, 1, products)
    far, products = lax.optimization_barrier((far, products))
    kept, *sent = products
    pieces = [own, below, above, *far]
    pieces += [lax.ppermute(piece, "dp", OTHER_CORE) for piece in pieces]
    rows, gram, energy, projected = dots(pieces, queries)

    energies = [lax.ppermute(energy, "layer", ring(4, d)) for d in (1, 2, 3)]
    beside = lax.ppermute(projected, "query", BESIDE)
    across = lax.ppermute(projected, "query", ACROSS)
    projections = [projected, beside, across, lax.ppermute(beside, "query", ACROSS)]

    energies, sent = lax.optimization_barrier((energies, sent))
    energies = [energy, *energies]
    taken = [lax.ppermute(part, "layer", ring(4, d)) for d, part in zip((1, 2, 3), sent)]
    solved = solve(gram, energies, rows, train, ratio)

    taken, solved, projections = lax.optimization_barrier((taken, solved, projections))
    plain = kept
    for part in taken:
        plain = plain + part.astype(jnp.float32)
    plain_sent = plain.astype(jnp.bfloat16)
    before = lax.ppermute(plain_sent, "query", ring(4, 1))
    after = lax.ppermute(plain_sent, "query", ring(4, 3))
    solved, plain_sent = lax.optimization_barrier((solved, plain_sent))

    fix, *fix_sent = pair_tiles(where, pairs, counts, energies, solved, projections, ratio)
    fixes = [lax.ppermute(f, "layer", ring(4, d)) for d, f in zip((1, 2, 3), fix_sent)]
    before, after, fix = lax.optimization_barrier((before, after, fix))
    half = before.shape[0] // 2
    low = lax.ppermute(before[:half], "query", ring(4, 1))
    high = lax.ppermute(after[half:], "query", ring(4, 3))
    plains = [plain, before, after, low, high]
    result = select(where, pairs, counts, energies, plains, ratio)
    for part in fixes:
        fix = fix + part.astype(jnp.float32)
    return result - fix


def solution(mesh):
    placed = (
        P("dp", "layer", None),
        P("query", None, "layer", None),
        P("dp", "layer", None),
        P(("dp", "query"), None),
        P("dp"),
    )
    return jax.shard_map(
        local,
        mesh=mesh,
        in_specs=placed,
        out_specs=P(("dp", "query"), "layer", None),
        check_vma=False,
    )
```

```python
import functools

import jax
import jax.numpy as jnp
from jax import lax
from jax.experimental import pallas as pl
from jax.experimental.pallas import tpu as pltpu
from jax.sharding import PartitionSpec as P

damp_ratio = 0.1
TILE = 128
VMEM_BYTES = 56 * 1024 * 1024
NT = (((1,), (1,)), ((), ()))


def whole():
    return pl.BlockSpec(memory_space=pltpu.VMEM)


def in_smem():
    return pl.BlockSpec(memory_space=pltpu.SMEM)


def params():
    return pltpu.CompilerParams(vmem_limit_bytes=VMEM_BYTES)


def cost(flops, nbytes):
    return pl.CostEstimate(flops=flops, bytes_accessed=nbytes, transcendentals=0)


def invert_tile(a, beside):
    n = a.shape[0]
    lane = lax.broadcasted_iota(jnp.int32, (n, n), 1)
    sub = lax.broadcasted_iota(jnp.int32, (n, n), 0)
    row_lane = lane[:1]
    for k in range(0, n, 4):
        beside(k // 4)
        col = [jnp.broadcast_to(a[:, k + i : k + i + 1], (n, n)) for i in range(4)]
        row = [a[k + i : k + i + 1, :] for i in range(4)]

        def entry(i, j):
            return jnp.broadcast_to(a[k + i : k + i + 1, k + j : k + j + 1], (1, n))

        p00, p01, p11 = entry(0, 0), entry(0, 1), entry(1, 1)
        q00, q01, q10, q11 = entry(2, 0), entry(2, 1), entry(3, 0), entry(3, 1)
        r00, r01, r11 = entry(2, 2), entry(2, 3), entry(3, 3)
        det = 1.0 / (p00 * p11 - p01 * p01)
        u00, u01, u11 = p11 * det, -p01 * det, p00 * det
        t00, t01 = q00 * u00 + q01 * u01, q00 * u01 + q01 * u11
        t10, t11 = q10 * u00 + q11 * u01, q10 * u01 + q11 * u11
        s00 = r00 - (t00 * q00 + t01 * q01)
        s01 = r01 - (t00 * q10 + t01 * q11)
        s11 = r11 - (t10 * q10 + t11 * q11)
        det = 1.0 / (s00 * s11 - s01 * s01)
        v00, v01, v11 = s11 * det, -s01 * det, s00 * det
        w00, w01 = v00 * t00 + v01 * t10, v00 * t01 + v01 * t11
        w10, w11 = v01 * t00 + v11 * t10, v01 * t01 + v11 * t11
        g00 = u00 + t00 * w00 + t10 * w10
        g01 = u01 + t00 * w01 + t10 * w11
        g11 = u11 + t01 * w01 + t11 * w11
        inv = [
            [g00, g01, -w00, -w10],
            [g01, g11, -w01, -w11],
            [-w00, -w01, v00, v01],
            [-w10, -w11, v01, v11],
        ]
        in_lane = (row_lane >= k) & (row_lane < k + 4)
        in_sub = (sub >= k) & (sub < k + 4)
        unit = [
            jnp.where(in_lane, jnp.where(row_lane == k + i, 1.0, 0.0), row[i]) for i in range(4)
        ]
        scaled = [
            inv[i][0] * unit[0] + inv[i][1] * unit[1] + inv[i][2] * unit[2] + inv[i][3] * unit[3]
            for i in range(4)
        ]
        left = [jnp.where(in_sub, jnp.where(sub == k + i, -1.0, 0.0), col[i]) for i in range(4)]
        a = jnp.where(((lane >= k) & (lane < k + 4)) | in_sub, 0.0, a)
        a = a - left[0] * scaled[0] - left[1] * scaled[1] - left[2] * scaled[2] - left[3] * scaled[3]
    return a


def full_dot(x, y):
    return jnp.dot(x, y, preferred_element_type=jnp.float32, precision=lax.Precision.HIGHEST)


def solve_kernel(
    ratio, gram_ref, e0, e1, e2, e3, rows_ref, train_hbm, out_ref, train_ref, cross_ref, train_sems
):
    n = gram_ref.shape[0]
    blocks = n // TILE
    step = train_ref.shape[0] // blocks
    train_copies = [
        pltpu.make_async_copy(
            train_hbm.at[pl.ds(r * step, step), :],
            train_ref.at[pl.ds(r * step, step), :],
            train_sems.at[r],
        )
        for r in range(blocks)
    ]
    for copy in train_copies:
        copy.start()
    energy = (e0[...] + e1[...] + e2[...] + e3[...])[:1, :1]
    scale = 1.0 / energy
    diag = lax.broadcasted_iota(jnp.int32, (n, n), 0) == lax.broadcasted_iota(jnp.int32, (n, n), 1)
    full = gram_ref[...] * scale + jnp.where(diag, ratio, 0.0)
    slabs = [full[i * TILE : (i + 1) * TILE] for i in range(blocks)]
    lane_block = lax.broadcasted_iota(jnp.int32, (TILE, n), 1) // TILE
    chunk = rows_ref.shape[1] // 16

    for k in range(blocks):
        part = slice(k * TILE, (k + 1) * TILE)
        held = slice(k * step, (k + 1) * step)
        train_copies[k].wait()

        def beside(s, k=k, held=held):
            if s % 2:
                return
            piece = s // 2
            depth = slice(piece * chunk, (piece + 1) * chunk)
            prod = lax.dot_general(
                train_ref[held, depth], rows_ref[:, depth], NT, preferred_element_type=jnp.float32
            )
            if piece == 0:
                cross_ref[held, :] = prod
            else:
                cross_ref[held, :] += prod

        tile_inv = invert_tile(slabs[k][:, part], beside)
        new = full_dot(tile_inv, jnp.where(lane_block == k, 0.0, slabs[k]))
        new = jnp.concatenate(
            [tile_inv if j == k else new[:, j * TILE : (j + 1) * TILE] for j in range(blocks)],
            axis=1,
        )
        for d in range(1, blocks):
            i = (k + d) % blocks
            slabs[i] = jnp.where(lane_block == k, 0.0, slabs[i]) - full_dot(slabs[i][:, part], new)
        slabs[k] = new
    x = jnp.concatenate(slabs, axis=0)
    hi = x.astype(jnp.bfloat16)
    x = x - hi.astype(jnp.float32)
    mid = x.astype(jnp.bfloat16)
    lo = (x - mid.astype(jnp.float32)).astype(jnp.bfloat16)
    for k in range(blocks):
        held = slice(k * step, (k + 1) * step)
        left = cross_ref[held, :]
        left_hi = left.astype(jnp.bfloat16)
        left_lo = (left - left_hi.astype(jnp.float32)).astype(jnp.bfloat16)
        prod = jnp.dot(left_hi, lo, preferred_element_type=jnp.float32)
        prod += jnp.dot(left_hi, mid, preferred_element_type=jnp.float32)
        prod += jnp.dot(left_lo, hi, preferred_element_type=jnp.float32)
        prod += jnp.dot(left_hi, hi, preferred_element_type=jnp.float32)
        out_ref[held, :] = (prod * scale).astype(jnp.bfloat16)


def solve(gram, energies, sketch_rows, train, ratio):
    n = gram.shape[0]
    rows, depth = train.shape
    return pl.pallas_call(
        functools.partial(solve_kernel, ratio),
        out_shape=jax.ShapeDtypeStruct((rows, n), jnp.bfloat16),
        in_specs=[whole()] * 6 + [pl.BlockSpec(memory_space=pl.ANY)],
        out_specs=whole(),
        scratch_shapes=[
            pltpu.VMEM((rows, depth), jnp.bfloat16),
            pltpu.VMEM((rows, n), jnp.float32),
            pltpu.SemaphoreType.DMA((n // TILE,)),
        ],
        compiler_params=params(),
        cost_estimate=cost(40_000_000_000, 30_000_000),
        name="solve",
    )(gram, *energies, sketch_rows, train)


def cross_kernel(given, where_ref, t_ref, q_ref, *refs):
    o0, o1, o2, o3, acc = refs[given:]
    groups, parts, rows, width = acc.shape
    prod = lax.dot_general(t_ref[...], q_ref[...], NT, preferred_element_type=jnp.float32)
    acc[...] = prod.reshape(groups, parts, rows, width)
    own = where_ref[1]
    for j, out in enumerate((o0, o1, o2, o3)):
        part = lax.rem(own + j, parts)
        out[...] = acc[:, part].astype(out.dtype)


def cross(where, train, queries, start, steps, filled=()):
    rows, depth = train.shape
    width = queries.shape[0]
    step = 512
    groups = step // TILE
    kept = TILE // 4
    out = (rows // TILE, kept, width)
    return pl.pallas_call(
        functools.partial(cross_kernel, len(filled)),
        grid=(steps,),
        in_specs=[
            in_smem(),
            pl.BlockSpec((step, depth), lambda i: (start + i, 0)),
            pl.BlockSpec((width, depth), lambda i: (0, 0)),
        ]
        + [pl.BlockSpec(memory_space=pl.ANY)] * len(filled),
        out_specs=[pl.BlockSpec((groups, kept, width), lambda i: (start + i, 0, 0))] * 4,
        out_shape=[jax.ShapeDtypeStruct(out, jnp.float32)]
        + [jax.ShapeDtypeStruct(out, jnp.bfloat16)] * 3,
        scratch_shapes=[pltpu.VMEM((groups, 4, kept, width), jnp.float32)],
        input_output_aliases={3 + j: j for j in range(len(filled))},
        compiler_params=params(),
        cost_estimate=cost(2 * steps * step * depth * width, 2 * (steps * step + width) * depth),
        name="cross",
    )(where, train, queries, *filled)


def dots_kernel(*refs):
    *pieces, q_ref, rows_ref, gram_ref, energy_ref, proj_ref, sums = refs
    k = pl.program_id(0)
    start = 0
    for piece in pieces:
        rows_ref[start : start + piece.shape[0], :] = piece[...]
        start += piece.shape[0]
    n = gram_ref.shape[0]
    rows = rows_ref[...]
    for part, left in ((slice(0, n), rows), (slice(n, None), q_ref[...])):
        prod = lax.dot_general(left, rows, NT, preferred_element_type=jnp.float32)
        sums[part, :] = jnp.where(k == 0, 0.0, sums[part, :]) + prod

    @pl.when(k == pl.num_programs(0) - 1)
    def _():
        gram = sums[:n, :]
        gram_ref[...] = gram
        proj_ref[...] = sums[n:, :].astype(jnp.bfloat16)
        diag = lax.broadcasted_iota(jnp.int32, (n, n), 0) == lax.broadcasted_iota(
            jnp.int32, (n, n), 1
        )
        trace = jnp.sum(jnp.where(diag, gram, 0.0))
        energy_ref[...] = jnp.full(energy_ref.shape, trace, jnp.float32)


def dots(pieces, queries):
    n = sum(piece.shape[0] for piece in pieces)
    width, depth = queries.shape
    chunk = 2048
    return pl.pallas_call(
        dots_kernel,
        grid=(depth // chunk,),
        in_specs=[
            pl.BlockSpec((piece.shape[0], chunk), lambda k: (0, k)) for piece in (*pieces, queries)
        ],
        out_specs=[pl.BlockSpec((n, chunk), lambda k: (0, k))] + [whole()] * 3,
        out_shape=[
            jax.ShapeDtypeStruct((n, depth), jnp.bfloat16),
            jax.ShapeDtypeStruct((n, n), jnp.float32),
            jax.ShapeDtypeStruct((8, 128), jnp.float32),
            jax.ShapeDtypeStruct((width, n), jnp.bfloat16),
        ],
        scratch_shapes=[pltpu.VMEM((n + width, n), jnp.float32)],
        compiler_params=params(),
        cost_estimate=cost(2 * n * depth * (n + width), 12_000_000),
        name="dots",
    )(*pieces, queries)


def tiles_kernel(
    ratio, where_ref, pairs_ref, counts_ref, e0, e1, e2, e3, solved, p0, p1, p2, p3,
    o0, o1, o2, o3, proj, tile,
):
    energy = (e0[...] + e1[...] + e2[...] + e3[...])[:1, :1]
    scale = 1.0 / (ratio * energy)
    for i, p in enumerate((p0, p1, p2, p3)):
        proj[i] = p[...].reshape(proj.shape[1:])
    first = where_ref[0]
    own_layer = where_ref[1]
    own_query = where_ref[2]
    unroll = tile.shape[0]
    row = lax.broadcasted_iota(jnp.int32, (TILE, TILE), 0)

    @pl.loop(0, pairs_ref.shape[0] // unroll)
    def _(g):
        for u in range(unroll):
            i = g * unroll + u
            block = pairs_ref[i, 0] - first
            query = pairs_ref[i, 1]
            place = lax.div(query, 4)
            second = jnp.where(place + own_query == 3, 2, 3)
            first_or_second = jnp.where(place == jnp.bitwise_xor(own_query, 1), 1, second)
            source = jnp.where(place == own_query, 0, first_or_second)
            left = solved[pl.ds(pl.multiple_of(block * TILE, TILE), TILE), :]
            right = proj[source, lax.rem(query, 4)]
            prod = lax.dot_general(left, right, NT, preferred_element_type=jnp.float32) * scale
            prod = jnp.where(row < counts_ref[block], prod, 0.0)
            tile[u] = prod.reshape(4, TILE // 4, TILE)
        for u in range(unroll):
            i = g * unroll + u
            for j, out in enumerate((o0, o1, o2, o3)):
                out[i] = tile[u, lax.rem(own_layer + j, 4)].astype(out.dtype)


def pair_tiles(where, pairs, counts, energies, solved, projections, ratio):
    count = pairs.shape[0]
    out = (count, TILE // 4, TILE)
    depth = solved.shape[1]
    return pl.pallas_call(
        functools.partial(tiles_kernel, ratio),
        in_specs=[in_smem()] * 3 + [whole()] * 9,
        out_specs=[whole()] * 4,
        out_shape=[jax.ShapeDtypeStruct(out, jnp.float32)]
        + [jax.ShapeDtypeStruct(out, jnp.bfloat16)] * 3,
        scratch_shapes=[
            pltpu.VMEM((4, 4, TILE, depth), jnp.bfloat16),
            pltpu.VMEM((16, 4, TILE // 4, TILE), jnp.float32),
        ],
        compiler_params=params(),
        cost_estimate=cost(1000, 1000),
        name="pair_tiles",
    )(where, pairs, counts, *energies, solved, *projections)


def select_kernel(
    ratio, where_ref, pairs_ref, counts_ref, e0, e1, e2, e3, g0, g1, g3, low, high, out_ref
):
    energy = (e0[...] + e1[...] + e2[...] + e3[...])[:1, :1]
    scale = 1.0 / (ratio * energy)
    first = where_ref[0]
    own_layer = where_ref[1]
    own_query = where_ref[2]
    count, rows, _ = out_ref.shape
    row = lax.broadcasted_iota(jnp.int32, out_ref.shape[1:], 0) + own_layer * rows
    half = low.shape[0]
    unroll = 8

    @pl.loop(0, count // unroll)
    def _(g):
        for u in range(unroll):
            i = g * unroll + u
            block = pairs_ref[i, 0] - first
            query = pairs_ref[i, 1]
            source = lax.rem(own_query - lax.div(query, 4) + 4, 4)
            column = pl.ds(pl.multiple_of(lax.rem(query, 4) * TILE, TILE), TILE)
            plain = g0[block, :, column]
            far = jnp.where(
                block < half,
                low[jnp.minimum(block, half - 1), :, column],
                high[jnp.maximum(block - half, 0), :, column],
            )
            for d, part in ((1, g1[block, :, column]), (2, far), (3, g3[block, :, column])):
                plain = jnp.where(source == d, part.astype(jnp.float32), plain)
            out_ref[i] = jnp.where(row < counts_ref[block], plain * scale, 0.0)


def select(where, pairs, counts, energies, plains, ratio):
    count = pairs.shape[0]
    return pl.pallas_call(
        functools.partial(select_kernel, ratio),
        in_specs=[in_smem()] * 3 + [whole()] * 9,
        out_specs=whole(),
        out_shape=jax.ShapeDtypeStruct((count, TILE // 4, TILE), jnp.float32),
        compiler_params=params(),
        cost_estimate=cost(1000, 1000),
        name="select",
    )(where, pairs, counts, *energies, *plains)


def ring(n, d):
    return [(i, (i + d) % n) for i in range(n)]


def chip_ring(d):
    return [(i, (i // 2 + d) % 4 * 2 + i % 2) for i in range(8)]


OTHER_CORE = [(i, i ^ 1) for i in range(8)]
BESIDE = [(i, i ^ 1) for i in range(4)]
ACROSS = [(i, 3 - i) for i in range(4)]


def local(train_grad, query_grad, sketch, pairs, counts):
    layer_count = lax.axis_size("layer")
    feature_count = sketch.shape[2]
    ratio = damp_ratio / (layer_count * feature_count)
    first = lax.axis_index("dp") * counts.shape[0]
    where = jnp.stack([first, lax.axis_index("layer"), lax.axis_index("query")]).astype(jnp.int32)
    train = train_grad.reshape(-1, feature_count)
    queries = query_grad.reshape(-1, feature_count)
    own = sketch.reshape(-1, feature_count)

    below = lax.ppermute(own, "dp", chip_ring(1))
    above = lax.ppermute(own, "dp", chip_ring(3))
    products = cross(where, train, queries, 0, 3)
    below, above, products = lax.optimization_barrier((below, above, products))
    half = own.shape[0] // 2
    far = [
        lax.ppermute(below[:half], "dp", chip_ring(1)),
        lax.ppermute(above[half:], "dp", chip_ring(3)),
    ]
    products = cross(where, train, queries, 3, 1, products)
    far, products = lax.optimization_barrier((far, products))
    kept, *sent = products
    pieces = [own, below, above, *far]
    pieces += [lax.ppermute(piece, "dp", OTHER_CORE) for piece in pieces]
    rows, gram, energy, projected = dots(pieces, queries)

    energies = [lax.ppermute(energy, "layer", ring(4, d)) for d in (2, 1, 3)]
    beside = lax.ppermute(projected, "query", BESIDE)
    across = lax.ppermute(projected, "query", ACROSS)
    projections = [projected, beside, across, lax.ppermute(beside, "query", ACROSS)]

    energies, sent = lax.optimization_barrier((energies, sent))
    energies = [energy, *energies]
    taken = [lax.ppermute(part, "layer", ring(4, d)) for d, part in zip((1, 2, 3), sent)]
    solved = solve(gram, energies, rows, train, ratio)

    taken, solved, projections = lax.optimization_barrier((taken, solved, projections))
    plain = kept
    for part in taken:
        plain = plain + part.astype(jnp.float32)
    plain_sent = plain.astype(jnp.bfloat16)
    before = lax.ppermute(plain_sent, "query", ring(4, 1))
    after = lax.ppermute(plain_sent, "query", ring(4, 3))
    solved, plain_sent = lax.optimization_barrier((solved, plain_sent))

    fix, *fix_sent = pair_tiles(where, pairs, counts, energies, solved, projections, ratio)
    one, two, three = fix_sent
    fixes = [lax.ppermute(f, "layer", ring(4, d)) for d, f in ((2, two), (1, one), (3, three))]
    before, after, fix = lax.optimization_barrier((before, after, fix))
    half = before.shape[0] // 2
    low = lax.ppermute(before[:half], "query", ring(4, 1))
    high = lax.ppermute(after[half:], "query", ring(4, 3))
    plains = [plain, before, after, low, high]
    result = select(where, pairs, counts, energies, plains, ratio)
    for part in fixes:
        fix = fix + part.astype(jnp.float32)
    return result - fix


def solution(mesh):
    placed = (
        P("dp", "layer", None),
        P("query", None, "layer", None),
        P("dp", "layer", None),
        P(("dp", "query"), None),
        P("dp"),
    )
    return jax.shard_map(
        local,
        mesh=mesh,
        in_specs=placed,
        out_specs=P(("dp", "query"), "layer", None),
        check_vma=False,
    )
```
